256 devices in a mesh: row: 16 (over x_lo, y, core), col: 16 (over z, x_hi).
Axes of the slice: x: 4 (x_hi: 2, x_lo: 2; x = x_hi * 2 + x_lo), y: 4, z: 8, core: 2. Of those that a mesh axis runs over, the one named last changes fastest.
Arguments:
- candidates: bfloat16 [16384, 768], P(('row', 'col')), may hold values from -6 to 6
- targets: bfloat16 [32768, 768], P(('col', 'row')), may hold values from -6 to 6
- target_domain: int32 [32768], P(('col', 'row')), may hold values from 0 to 63
- domain_counts: int32 [64], replicated, may hold values from 1 to 999
Outputs:
- projection: bfloat16 [16384, 768], P(('row', 'col'))
- cand_potential: float32 [16384], P('row')
- tgt_potential: float32 [32768], P('col')
The draws below stay inside these ranges and needn't reach their ends.
All inputs are finite; a program needn't handle non-finite values.
Results may differ from the reference program's by a relative error of at most 0.023.
Values may be sent and summed in bfloat16 or wider, within the bound.
No kernel may reach another device: no remote copies, remote signals or barrier semaphores. Data moves between devices by JAX's collectives and lax.ppermute only.
A program may use at most 64 MiB of HBM per device.

```python
import math
import jax
import jax.numpy as jnp
import numpy as np
from jax import lax

D = 768
DOMAINS = 64
ITERS = 2
CAND_BLK = 1024
NC = 16384
NT = 32768


def touch_ends(result, key, least, high):
    shape = result.shape
    spot = [jax.random.randint(jax.random.fold_in(key, axis), (), 0, shape[axis]) for axis in range(len(shape))]
    result = result.at[tuple(spot)].set(least)
    longest = shape.index(max(shape))
    spot[longest] = (spot[longest] + 1) % shape[longest]
    return result.at[tuple(spot)].set(high)


def level_of(rng, shape, cuts, smallest, top_value):
    def one(dim, blocks):
        heights = jax.random.uniform(jax.random.fold_in(jax.random.fold_in(rng, 6), dim), (blocks,), jnp.float32, smallest / len(cuts), top_value / len(cuts))
        return jnp.repeat(jnp.exp(heights), shape[dim] // blocks).reshape((-1,) + (1,) * (len(shape) - dim - 1))

    loudness = one(*cuts[0])
    for cut in cuts[1:]:
        loudness = loudness * one(*cut)
    return loudness


def rank_table(number_of, slope):
    weights = [(1 << 20) // math.isqrt(rank ** slope) + 1 for rank in range(1, number_of + 1)]
    spread = 1 + sum(weights) // (1 << 30)
    return np.cumsum(np.array([max(1, weight // spread) for weight in weights]))


def ranked_ids(stream_key, extent, number_of, slope):
    listing = rank_table(number_of, slope)
    pick = jax.random.randint(jax.random.fold_in(stream_key, 1), extent, 0, int(listing[number_of - 1]))
    rank = jnp.searchsorted(jnp.asarray(listing, jnp.int32), pick, side="right")
    return jax.random.permutation(jax.random.fold_in(stream_key, 2), number_of)[rank].astype(jnp.int32)


def scatter_about(rng, dims, spread, most, split=(), dtype=jnp.bfloat16):
    array = spread * jax.random.normal(rng, dims, jnp.float32)
    if split:
        array = array * level_of(rng, dims, split, -0.22, 0.18)
    return jnp.clip(array, -most, most).astype(dtype)


def setup_inputs(seed: int = 0) -> dict:
    key_of = jax.random.split(jax.random.key(seed), 5)
    candidates = scatter_about(key_of[0], (NC, D), 1.0, 6.0, ((0, 256),))
    targets = scatter_about(key_of[1], (NT, D), 1.0, 6.0, ((0, 256),))
    target_domain = touch_ends(ranked_ids(key_of[2], (NT,), DOMAINS, 2), jax.random.fold_in(key_of[2], 3), 0, DOMAINS - 1).astype(jnp.int32)
    domain_counts = touch_ends(jax.random.randint(key_of[3], (DOMAINS,), 1, 1000), jax.random.fold_in(key_of[3], 1), 1, 999).astype(jnp.int32)
    return {"candidates": candidates, "targets": targets, "target_domain": target_domain, "domain_counts": domain_counts}


eps = 0.01


def reference(candidates, targets, target_domain, domain_counts):
    total_rows = candidates.shape[0]
    total_cols = targets.shape[0]
    sqx = jnp.sum(jnp.square(candidates.astype(jnp.float32)), axis=1)
    sqy = jnp.sum(jnp.square(targets.astype(jnp.float32)), axis=1)
    counts = domain_counts.astype(jnp.float32)
    weight = counts[target_domain]
    logb = jnp.log(weight / jnp.sum(counts)) + jnp.log(jnp.float32(domain_counts.shape[0])) - jnp.log(jnp.float32(total_cols))
    loga = -jnp.log(jnp.float32(total_rows))
    blocks = candidates.reshape(total_rows // CAND_BLK, CAND_BLK, D)
    sq_blocks = sqx.reshape(total_rows // CAND_BLK, CAND_BLK)

    def tile(xb, sb):
        cross = lax.dot_general(xb, targets, (((1,), (1,)), ((), ())), preferred_element_type=jnp.float32)
        return (sb[:, None] + sqy[None, :] - 2.0 * cross) / D

    def cand_update(cost, tgt_pot):
        return eps * loga - eps * jax.nn.logsumexp((tgt_pot[None, :] - cost) / eps, axis=1)

    def sweep(tgt_pot):
        def step(carry, item):
            run_max, run_sum = carry
            xb, sb = item
            cost = tile(xb, sb)
            cand = cand_update(cost, tgt_pot)
            scores = (cand[:, None] - cost) / eps
            new_max = jnp.maximum(run_max, jnp.max(scores, axis=0))
            run_sum = run_sum * jnp.exp(run_max - new_max) + jnp.sum(jnp.exp(scores - new_max[None, :]), axis=0)
            return (new_max, run_sum), cand

        init = (jnp.full(sqy.shape, -jnp.inf, jnp.float32), jnp.zeros(sqy.shape, jnp.float32))
        (run_max, run_sum), cand = lax.scan(step, init, (blocks, sq_blocks))
        return cand.reshape(-1), eps * logb - eps * (run_max + jnp.log(run_sum))

    tgt_pot = jnp.zeros(sqy.shape, jnp.float32)
    for it in range(ITERS):
        cand_pot, tgt_pot = sweep(tgt_pot)

    def final(carry, item):
        xb, sb = item
        cost = tile(xb, sb)
        cand = cand_update(cost, tgt_pot)
        plan = jnp.exp((cand[:, None] + tgt_pot[None, :] - cost) / eps - loga).astype(jnp.bfloat16)
        proj = jnp.dot(plan, targets, preferred_element_type=jnp.float32).astype(jnp.bfloat16)
        return carry, (proj, cand)

    unused, (proj, cand) = lax.scan(final, jnp.float32(0.0), (blocks, sq_blocks))
    return proj.reshape(total_rows, D), cand.reshape(-1), tgt_pot
```

```python
import functools
import math

import jax
import jax.numpy as jnp
from jax import lax
from jax.experimental import pallas as pl
from jax.experimental.pallas import tpu as pltpu
from jax.sharding import Mesh, PartitionSpec as P

eps = 0.01
LOG2E = math.log2(math.e)
TO2 = LOG2E / eps

ROW = ("xl", "y", "core")
COL = ("z", "xh")
CG = ("xh", "xl", "y")
TG = ("core", "z")
RING = (0, -1, -2, -3, 1, 2, 3, 4)
LANE = 128
SUB = 64
BLK = 256
MIB = 1024 * 1024
VMEM_LIMIT = 30 * MIB


def spread(row):
    return jnp.broadcast_to(row, (LANE, LANE)).T


def fold_lanes(m, l):
    mt, lt = m.T, l.T
    top = jnp.max(mt, axis=0, keepdims=True)
    return top + jnp.log2(jnp.sum(lt * jnp.exp2(mt - top), axis=0, keepdims=True))


def merge(parts):
    top = jnp.max(parts, axis=0)
    return top + jnp.log2(jnp.sum(jnp.exp2(parts - top[None]), axis=0))


def copies(out_ref, at, value):
    for d in range(out_ref.shape[0]):
        out_ref[d, pl.ds(at, 1), :] = value


def spread_kernel(x_ref, out_ref, sems):
    started = []
    for d in range(out_ref.shape[0]):
        copy = pltpu.make_async_copy(x_ref, out_ref.at[d], sems.at[d])
        copy.start()
        started.append(copy)
    for copy in started:
        copy.wait()


def norms(scale, x_ref, out_ref):
    for r in range(0, x_ref.shape[0], LANE):
        acc = jnp.zeros((LANE, LANE), jnp.float32)
        for k in range(0, x_ref.shape[1], LANE):
            x = x_ref[pl.ds(r, LANE), pl.ds(k, LANE)].astype(jnp.float32)
            acc = acc + x * x
        total = jnp.sum(acc, axis=1, keepdims=True) * scale
        out_ref[pl.ds(r, LANE), :] = jnp.broadcast_to(total, (LANE, LANE))


def half_cost(scale, x_ref, sqx_ref, y_ref, c_ref, m_ref, l_ref):
    rows, half = c_ref.shape
    tiles = half // LANE
    sqy = []
    for t in range(tiles):
        acc = jnp.zeros((LANE, LANE), jnp.float32)
        for k in range(0, y_ref.shape[1], LANE):
            y = y_ref[pl.ds(t * LANE, LANE), pl.ds(k, LANE)].astype(jnp.float32)
            acc = acc + y * y
        sqy.append(jnp.sum(acc.T, axis=0, keepdims=True) * scale)
    wide = 512
    for b in range(0, rows, BLK):
        x = x_ref[pl.ds(b, BLK), :]
        for at in range(0, half, wide):
            cross = lax.dot_general(
                x, y_ref[pl.ds(at, wide), :], (((1,), (1,)), ((), ())), preferred_element_type=jnp.float32
            )
            for r in range(0, BLK, SUB):
                here = pl.ds(b + r, SUB)
                sqx = sqx_ref[here, :]
                low = l_ref[here, :] if at else None
                for k in range(wide // LANE):
                    t = at // LANE + k
                    part = cross[r : r + SUB, k * LANE : (k + 1) * LANE]
                    cost = (sqx + sqy[t]) - (2.0 * scale) * part
                    c_ref[here, pl.ds(t * LANE, LANE)] = cost
                    low = cost if low is None else jnp.minimum(low, cost)
                l_ref[here, :] = low
        for r in range(b, b + BLK, SUB):
            here = pl.ds(r, SUB)
            low = l_ref[here, :]
            l = jnp.zeros((SUB, LANE), jnp.float32)
            for t in range(tiles):
                l = l + jnp.exp2(low - c_ref[here, pl.ds(t * LANE, LANE)])
            m_ref[here, :] = -low
            l_ref[here, :] = l


def first_cost(scale, x_ref, y_ref, c_ref, m_ref, l_ref, sqx_ref):
    norms(scale, x_ref, sqx_ref)
    half_cost(scale, x_ref, sqx_ref, y_ref, c_ref, m_ref, l_ref)


def place(tile):
    n = len(RING)
    core = lax.rem(tile // n + lax.axis_index("core"), 2)
    return core * n + lax.rem(lax.axis_index("z") + RING[tile % n] + n, n)


def second_cost(scale, x_ref, sqx_ref, y_ref, m0_ref, l0_ref, c_ref, out_ref, m_ref, l_ref):
    half_cost(scale, x_ref, sqx_ref, y_ref, c_ref, m_ref, l_ref)
    for k in range(c_ref.shape[0] // LANE):
        here = pl.ds(k * LANE, LANE)
        m0, m1 = m0_ref[here, :], m_ref[here, :]
        m = jnp.maximum(m0, m1)
        l = l0_ref[here, :] * jnp.exp2(m0 - m) + l_ref[here, :] * jnp.exp2(m1 - m)
        copies(out_ref, k, fold_lanes(m, l))


def col_kernel(log2a, parts_ref, ca_ref, cb_ref, *refs):
    *logb_ref, out_ref, u_ref = refs
    rows, half = ca_ref.shape
    total = 2 * half // LANE
    if logb_ref:
        copies(out_ref, total, logb_ref[0][...])
        for k in range(total + 1, out_ref.shape[1]):
            copies(out_ref, k, jnp.zeros((1, LANE), jnp.float32))
    u = log2a - merge(parts_ref[...])
    for k in range(rows // LANE):
        u_ref[pl.ds(k * LANE, LANE), :] = spread(u[k : k + 1, :])
    sub, group = 32, 4
    for h, c_ref in enumerate((ca_ref, cb_ref)):
        for k0 in range(0, half // LANE, group):
            ks = range(k0, k0 + group)

            def score(r, k):
                return u_ref[pl.ds(r, sub), :] - c_ref[pl.ds(r, sub), pl.ds(k * LANE, LANE)]

            def top_step(i, m):
                r = pl.multiple_of(i * sub, sub)
                return tuple(jnp.maximum(a, score(r, k)) for a, k in zip(m, ks))

            def sum_step(m, i, l):
                r = pl.multiple_of(i * sub, sub)
                return tuple(a + jnp.exp2(score(r, k) - b) for a, b, k in zip(l, m, ks))

            m = lax.fori_loop(1, rows // sub, top_step, tuple(score(0, k) for k in ks), unroll=4)
            zero = jnp.zeros((sub, LANE), jnp.float32)
            l = lax.fori_loop(
                0, rows // sub, functools.partial(sum_step, m), (zero,) * group, unroll=4
            )
            for a, b, k in zip(l, m, ks):
                top = jnp.max(b, axis=0, keepdims=True)
                e = top + jnp.log2(jnp.sum(a * jnp.exp2(b - top), axis=0, keepdims=True))
                copies(out_ref, place(h * (total // 2) + k), e)


def tgt_pot(parts, logb_ref, v_ref, pot_ref):
    pot_ref[...] = logb_ref[...] - merge(parts)
    for t in range(v_ref.shape[0]):
        v_ref[pl.ds(t, 1), :] = pot_ref[pl.ds(place(t), 1), :]


def scores(v_ref, ca_ref, cb_ref, here):
    tiles = ca_ref.shape[1] // LANE

    def score(t):
        ref = ca_ref if t < tiles else cb_ref
        return v_ref[pl.ds(t, 1), :] - ref[here, pl.ds((t % tiles) * LANE, LANE)]

    return score, 2 * tiles


def row_kernel(parts_ref, ca_ref, cb_ref, out_ref, logb_ref, v_ref, pot_ref, m_ref, l_ref):
    rows = ca_ref.shape[0]
    total = v_ref.shape[0]
    for d in range(total):
        logb_ref[pl.ds(d, 1), :] = parts_ref[d, pl.ds(total, 1), :]
    tgt_pot(parts_ref[:, pl.ds(0, total), :], logb_ref, v_ref, pot_ref)

    def body(i, carry):
        here = pl.ds(pl.multiple_of(i * LANE, LANE), LANE)
        score, tiles = scores(v_ref, ca_ref, cb_ref, here)
        m = score(0)
        for t in range(1, tiles):
            m = jnp.maximum(m, score(t))
        l = jnp.zeros((LANE, LANE), jnp.float32)
        for t in range(tiles):
            l = l + jnp.exp2(score(t) - m)
        m_ref[here, :] = m
        l_ref[here, :] = l
        return carry

    lax.fori_loop(0, rows // LANE, body, 0)
    for k in range(rows // LANE):
        here = pl.ds(k * LANE, LANE)
        copies(out_ref, k, fold_lanes(m_ref[here, :], l_ref[here, :]))


def plan_kernel(parts_ref, logb_ref, ca_ref, cb_ref, ya_ref, yb_ref, out_ref, p_ref, v_ref, pot_ref, plan_ref, held_ref, sems):
    rows, half = ca_ref.shape
    tgt_pot(parts_ref[...], logb_ref, v_ref, pot_ref)
    first = 2 * rows // LANE
    n = pot_ref.shape[0] // 2
    for h in range(2):
        copies(out_ref, first + h, pot_ref[pl.ds(lax.axis_index("z") + h * n, 1), :])
    for k in range(first + 2, out_ref.shape[1]):
        copies(out_ref, k, jnp.zeros((1, LANE), jnp.float32))

    leaving = []
    for k in range(rows // LANE):
        here = pl.ds(k * LANE, LANE)
        score, tiles = scores(v_ref, ca_ref, cb_ref, here)
        m = score(0)
        for t in range(1, tiles):
            m = jnp.maximum(m, score(t))
        m = jnp.broadcast_to(jnp.max(m, axis=1, keepdims=True), (LANE, LANE))
        l = jnp.zeros((LANE, LANE), jnp.float32)
        for t in range(tiles):
            p = jnp.exp2(score(t) - m)
            l = l + p
            plan_ref[here, pl.ds(t * LANE, LANE)] = p.astype(jnp.bfloat16)
        m = m.T[:1, :]
        l = jnp.sum(l.T, axis=0, keepdims=True)
        copies(out_ref, k, m + jnp.log2(l))
        copies(out_ref, rows // LANE + k, m)
        if (k + 1) * LANE % BLK == 0:
            here = pl.ds((k + 1) * LANE - BLK, BLK)
            total = jnp.dot(plan_ref[here, pl.ds(0, half)], ya_ref[...], preferred_element_type=jnp.float32)
            total = total + jnp.dot(
                plan_ref[here, pl.ds(half, half)], yb_ref[...], preferred_element_type=jnp.float32
            )
            held_ref[here, :] = total.astype(jnp.bfloat16)
            copy = pltpu.make_async_copy(held_ref.at[here], p_ref.at[here], sems.at[k * LANE // BLK])
            copy.start()
            leaving.append(copy)
    for copy in leaving:
        copy.wait()


def last_kernel(log2a, share, parts_ref, gain_ref, cand_ref, tgt_ref):
    top = share * lax.axis_size(CG) // LANE
    per = LANE // share
    per_xh = top // lax.axis_size("xh")
    mine = lax.axis_index(("xl", "y"))
    lane = lax.broadcasted_iota(jnp.int32, (1, LANE), 1) // share
    lse = merge(parts_ref[:, pl.ds(0, top), :])
    cand_ref[...] = jnp.zeros(cand_ref.shape, jnp.float32)
    row_of = lax.broadcasted_iota(jnp.int32, lse.shape, 0)

    def row(value, at):
        return jnp.sum(jnp.where(row_of == at, value, 0.0), axis=0, keepdims=True)

    def shifted(value, to, at):
        out = jnp.zeros_like(value)
        for off in range(per):
            moved = pltpu.roll(value, ((to - off) % per) * share, 1) if (to - off) % per else value
            out = jnp.where(at == off, moved, out)
        return out

    pieces = jnp.zeros((1, LANE), jnp.float32)
    for h in range(lax.axis_size("xh")):
        value = shifted(row(lse, h * per_xh + mine // per), h, lax.rem(mine, per))
        pieces = jnp.where(lane == h, value, pieces)
    cand_ref[pl.ds(lax.axis_index("z"), 1), :] = (log2a - pieces) / TO2

    me = lax.axis_index(CG)
    own = parts_ref[:, pl.ds(top + me // per, 1), :].reshape(parts_ref.shape[0], LANE)
    gain_ref[...] = shifted(jnp.exp2(own - row(lse, me // per)), 0, lax.rem(me, per))

    n = lax.axis_size(("xl", "y"))
    for k in range(n):
        pair = parts_ref[lax.axis_index("xh") * n + k, pl.ds(2 * top, 2), :]
        tgt_ref[pl.ds(2 * k, 2), :] = pair / TO2


VMEM = pl.BlockSpec(memory_space=pltpu.VMEM)
HBM = pl.BlockSpec(memory_space=pltpu.HBM)


def local(candidates, targets, target_domain, domain_counts):
    f32, bf16 = jnp.float32, jnp.bfloat16
    width = candidates.shape[1]
    plane = lax.axis_size(CG)
    pairs = lax.axis_size(TG)
    depth = lax.axis_size("z")
    share = candidates.shape[0]
    rows = share * plane
    half = targets.shape[0] * depth
    cols = 2 * half
    total_rows = rows * pairs
    total_cols = cols * plane

    def run(kernel, args, outs, scratch=(), special=()):
        special = dict(special)
        return pl.pallas_call(
            kernel,
            in_specs=[special.get(i, VMEM) for i in range(len(args))],
            out_specs=[o[2] if len(o) > 2 else VMEM for o in outs],
            out_shape=[(pltpu.HBM if len(o) > 2 else jax.ShapeDtypeStruct)(o[0], o[1]) for o in outs],
            scratch_shapes=[pltpu.VMEM(*v) if isinstance(v, tuple) else v for v in scratch],
            compiler_params=pltpu.CompilerParams(vmem_limit_bytes=VMEM_LIMIT),
            cost_estimate=pl.CostEstimate(flops=rows * cols * width, bytes_accessed=4 * rows * cols, transcendentals=rows * cols),
        )(*[pltpu.with_memory_space_constraint(a, pltpu.HBM) if special.get(i) is HBM else a for i, a in enumerate(args)])

    def shift(block, by):
        return lax.ppermute(block, "z", [(i, (i + by) % depth) for i in range(depth)])

    (x,) = run(
        spread_kernel,
        (candidates,),
        [((plane, share, width), bf16, HBM)],
        [pltpu.SemaphoreType.DMA((plane,))],
    )
    x = lax.all_to_all(x, CG, 0, 0, tiled=True).reshape(rows, width)
    up, down = [targets], [targets]
    for _ in range(depth // 2 - 1):
        up.append(shift(up[-1], 1))
        down.append(shift(down[-1], -1))
    mid = targets.shape[0] // 2
    ends = [shift(up[-1][:mid], 1), shift(down[-1][mid:], -1)]
    ya = jnp.concatenate(up + down[1:] + ends, axis=0)
    counts = domain_counts.astype(f32)
    domains = jnp.arange(domain_counts.shape[0], dtype=jnp.int32)
    weight = jnp.sum(jnp.where(target_domain[:, None] == domains[None, :], counts[None, :], 0.0), axis=1)
    logb = jnp.log2(weight / jnp.sum(counts)) + (
        math.log2(domain_counts.shape[0]) - math.log2(total_cols)
    )
    scale = TO2 / width
    ya, x, logb = lax.optimization_barrier((ya, x, logb[None, :]))
    yb = lax.ppermute(ya, "core", [(0, 1), (1, 0)])

    log2a = -math.log2(total_rows)
    row_shape = ((plane, rows // LANE, LANE), f32)
    col_shape = ((pairs, cols // LANE, LANE), f32)
    wide_shape = ((pairs, cols // LANE + 8, LANE), f32)
    last_shape = ((plane, 2 * rows // LANE + 8, LANE), f32)
    stat = ((rows, LANE), f32)
    vec = ((cols // LANE, LANE), f32)
    chalf = ((rows, half), f32)
    ca, m, l, sqx = run(functools.partial(first_cost, scale), (x, ya), [chalf, stat, stat, stat])
    cb, out = run(
        functools.partial(second_cost, scale), (x, sqx, yb, m, l), [chalf, row_shape], [stat, stat]
    )

    def columns(out, shape, *extra):
        parts = lax.all_to_all(out, CG, 0, 0, tiled=True)
        (out,) = run(functools.partial(col_kernel, log2a), (parts, ca, cb, *extra), [shape], [stat])
        return lax.all_to_all(out, TG, 0, 0, tiled=True)

    out, logb = run(
        row_kernel, (columns(out, wide_shape, logb), ca, cb), [row_shape, vec], [vec, vec, stat, stat]
    )
    out, partial = run(
        plan_kernel,
        (columns(out, col_shape), logb, ca, cb, ya, yb),
        [last_shape, ((rows, width), bf16, HBM)],
        [vec, vec, ((rows, cols), bf16), ((rows, width), bf16), pltpu.SemaphoreType.DMA((rows // BLK,))],
    )
    parts = lax.all_to_all(out, CG, 0, 0, tiled=True)
    moved = lax.all_to_all(partial.reshape(plane, share, width), CG, 0, 0, tiled=True)
    gain, cand, tgt = run(
        functools.partial(last_kernel, log2a, share),
        (parts,),
        [((plane, LANE), f32), ((depth, LANE), f32), vec],
    )
    projection = jnp.sum(moved.astype(f32) * gain[:, :share, None], axis=0).astype(bf16)
    for bit in (1, 2, 4):
        cand = cand + lax.ppermute(cand, "z", [(i, i ^ bit) for i in range(depth)])
    return projection, cand.reshape(-1), tgt.reshape(-1)


def solution(mesh):
    fine = Mesh(mesh.devices.reshape(2, -1, 2, mesh.shape["col"] // 2, 2), ROW + COL)
    tgt = P(COL + ROW)
    return jax.shard_map(
        local,
        mesh=fine,
        in_specs=(P(ROW + COL, None), P(COL + ROW, None), tgt, P()),
        out_specs=(P(ROW + COL, None), P(ROW), P(COL)),
        check_vma=False,
    )
```

```python
import functools
import math

import jax
import jax.numpy as jnp
from jax import lax
from jax.experimental import pallas as pl
from jax.experimental.pallas import tpu as pltpu
from jax.sharding import Mesh, PartitionSpec as P

eps = 0.01
LOG2E = math.log2(math.e)
TO2 = LOG2E / eps

ROW = ("xl", "y", "core")
COL = ("z", "xh")
CG = ("xh", "xl", "y")
TG = ("core", "z")
RING = (0, -1, 1, -2, 2, -3, 3, 4)
LANE = 128
SUB = 64
BLK = 256
MIB = 1024 * 1024
VMEM_LIMIT = 30 * MIB


def spread(row):
    return jnp.broadcast_to(row, (LANE, LANE)).T


def fold_lanes(m, l):
    mt, lt = m.T, l.T
    top = jnp.max(mt, axis=0, keepdims=True)
    return top + jnp.log2(jnp.sum(lt * jnp.exp2(mt - top), axis=0, keepdims=True))


def merge(parts):
    top = jnp.max(parts, axis=0)
    return top + jnp.log2(jnp.sum(jnp.exp2(parts - top[None]), axis=0))


def copies(out_ref, at, value):
    for d in range(out_ref.shape[0]):
        out_ref[d, pl.ds(at, 1), :] = value


def spread_kernel(x_ref, out_ref, sems):
    started = []
    for d in range(out_ref.shape[0]):
        copy = pltpu.make_async_copy(x_ref, out_ref.at[d], sems.at[d])
        copy.start()
        started.append(copy)
    for copy in started:
        copy.wait()


def norms(scale, x_ref, out_ref):
    for r in range(0, x_ref.shape[0], LANE):
        acc = jnp.zeros((LANE, LANE), jnp.float32)
        for k in range(0, x_ref.shape[1], LANE):
            x = x_ref[pl.ds(r, LANE), pl.ds(k, LANE)].astype(jnp.float32)
            acc = acc + x * x
        total = jnp.sum(acc, axis=1, keepdims=True) * scale
        out_ref[pl.ds(r, LANE), :] = jnp.broadcast_to(total, (LANE, LANE))


def half_cost(scale, x_ref, sqx_ref, y_ref, c_ref, m_ref, l_ref):
    rows, half = c_ref.shape
    tiles = half // LANE
    sqy = []
    for t in range(tiles):
        acc = jnp.zeros((LANE, LANE), jnp.float32)
        for k in range(0, y_ref.shape[1], LANE):
            y = y_ref[pl.ds(t * LANE, LANE), pl.ds(k, LANE)].astype(jnp.float32)
            acc = acc + y * y
        sqy.append(jnp.sum(acc.T, axis=0, keepdims=True) * scale)
    wide = 512
    for b in range(0, rows, BLK):
        x = x_ref[pl.ds(b, BLK), :]
        for at in range(0, half, wide):
            cross = lax.dot_general(
                x, y_ref[pl.ds(at, wide), :], (((1,), (1,)), ((), ())), preferred_element_type=jnp.float32
            )
            for r in range(0, BLK, SUB):
                here = pl.ds(b + r, SUB)
                sqx = sqx_ref[here, :]
                low = l_ref[here, :] if at else None
                for k in range(wide // LANE):
                    t = at // LANE + k
                    part = cross[r : r + SUB, k * LANE : (k + 1) * LANE]
                    cost = (sqx + sqy[t]) - (2.0 * scale) * part
                    c_ref[here, pl.ds(t * LANE, LANE)] = cost
                    low = cost if low is None else jnp.minimum(low, cost)
                l_ref[here, :] = low
        for r in range(b, b + BLK, SUB):
            here = pl.ds(r, SUB)
            low = l_ref[here, :]
            l = jnp.zeros((SUB, LANE), jnp.float32)
            for t in range(tiles):
                l = l + jnp.exp2(low - c_ref[here, pl.ds(t * LANE, LANE)])
            m_ref[here, :] = -low
            l_ref[here, :] = l


def first_cost(scale, x_ref, y_ref, c_ref, m_ref, l_ref, sqx_ref):
    norms(scale, x_ref, sqx_ref)
    half_cost(scale, x_ref, sqx_ref, y_ref, c_ref, m_ref, l_ref)


def place(tile):
    n = len(RING)
    core = lax.rem(tile // n + lax.axis_index("core"), 2)
    return core * n + lax.rem(lax.axis_index("z") + RING[tile % n] + n, n)


def second_cost(scale, x_ref, sqx_ref, y_ref, m0_ref, l0_ref, c_ref, out_ref, m_ref, l_ref):
    half_cost(scale, x_ref, sqx_ref, y_ref, c_ref, m_ref, l_ref)
    for k in range(c_ref.shape[0] // LANE):
        here = pl.ds(k * LANE, LANE)
        m0, m1 = m0_ref[here, :], m_ref[here, :]
        m = jnp.maximum(m0, m1)
        l = l0_ref[here, :] * jnp.exp2(m0 - m) + l_ref[here, :] * jnp.exp2(m1 - m)
        copies(out_ref, k, fold_lanes(m, l))


def col_kernel(log2a, parts_ref, ca_ref, cb_ref, *refs):
    *logb_ref, out_ref, u_ref = refs
    rows, half = ca_ref.shape
    total = 2 * half // LANE
    if logb_ref:
        copies(out_ref, total, logb_ref[0][...])
        for k in range(total + 1, out_ref.shape[1]):
            copies(out_ref, k, jnp.zeros((1, LANE), jnp.float32))
    u = log2a - merge(parts_ref[...])
    for k in range(rows // LANE):
        u_ref[pl.ds(k * LANE, LANE), :] = spread(u[k : k + 1, :])
    sub, group = 32, 4
    for h, c_ref in enumerate((ca_ref, cb_ref)):
        for k0 in range(0, half // LANE, group):
            ks = range(k0, k0 + group)

            def score(r, k):
                return u_ref[pl.ds(r, sub), :] - c_ref[pl.ds(r, sub), pl.ds(k * LANE, LANE)]

            def top_step(i, m):
                r = pl.multiple_of(i * sub, sub)
                return tuple(jnp.maximum(a, score(r, k)) for a, k in zip(m, ks))

            def sum_step(m, i, l):
                r = pl.multiple_of(i * sub, sub)
                return tuple(a + jnp.exp2(score(r, k) - b) for a, b, k in zip(l, m, ks))

            m = lax.fori_loop(1, rows // sub, top_step, tuple(score(0, k) for k in ks), unroll=4)
            zero = jnp.zeros((sub, LANE), jnp.float32)
            l = lax.fori_loop(
                0, rows // sub, functools.partial(sum_step, m), (zero,) * group, unroll=4
            )
            for a, b, k in zip(l, m, ks):
                top = jnp.max(b, axis=0, keepdims=True)
                e = top + jnp.log2(jnp.sum(a * jnp.exp2(b - top), axis=0, keepdims=True))
                copies(out_ref, place(h * (total // 2) + k), e)


def tgt_pot(parts, logb_ref, v_ref, pot_ref):
    pot_ref[...] = logb_ref[...] - merge(parts)
    for t in range(v_ref.shape[0]):
        v_ref[pl.ds(t, 1), :] = pot_ref[pl.ds(place(t), 1), :]


def scores(v_ref, ca_ref, cb_ref, here):
    tiles = ca_ref.shape[1] // LANE

    def score(t):
        ref = ca_ref if t < tiles else cb_ref
        return v_ref[pl.ds(t, 1), :] - ref[here, pl.ds((t % tiles) * LANE, LANE)]

    return score, 2 * tiles


def row_kernel(parts_ref, ca_ref, cb_ref, out_ref, logb_ref, v_ref, pot_ref, m_ref, l_ref):
    rows = ca_ref.shape[0]
    total = v_ref.shape[0]
    for d in range(total):
        logb_ref[pl.ds(d, 1), :] = parts_ref[d, pl.ds(total, 1), :]
    tgt_pot(parts_ref[:, pl.ds(0, total), :], logb_ref, v_ref, pot_ref)

    def body(i, carry):
        here = pl.ds(pl.multiple_of(i * LANE, LANE), LANE)
        score, tiles = scores(v_ref, ca_ref, cb_ref, here)
        m = score(0)
        for t in range(1, tiles):
            m = jnp.maximum(m, score(t))
        l = jnp.zeros((LANE, LANE), jnp.float32)
        for t in range(tiles):
            l = l + jnp.exp2(score(t) - m)
        m_ref[here, :] = m
        l_ref[here, :] = l
        return carry

    lax.fori_loop(0, rows // LANE, body, 0)
    for k in range(rows // LANE):
        here = pl.ds(k * LANE, LANE)
        copies(out_ref, k, fold_lanes(m_ref[here, :], l_ref[here, :]))


def plan_kernel(parts_ref, logb_ref, ca_ref, cb_ref, ya_ref, yb_ref, out_ref, p_ref, v_ref, pot_ref, held_ref, sems):
    rows, half = ca_ref.shape
    tgt_pot(parts_ref[...], logb_ref, v_ref, pot_ref)
    first = 2 * rows // LANE
    n = pot_ref.shape[0] // 2
    for h in range(2):
        copies(out_ref, first + h, pot_ref[pl.ds(lax.axis_index("z") + h * n, 1), :])
    for k in range(first + 2, out_ref.shape[1]):
        copies(out_ref, k, jnp.zeros((1, LANE), jnp.float32))

    leaving = []
    for b in range(0, rows, BLK):
        plan = []
        for k in range(b // LANE, (b + BLK) // LANE):
            score, tiles = scores(v_ref, ca_ref, cb_ref, pl.ds(k * LANE, LANE))
            m = score(0)
            for t in range(1, tiles):
                m = jnp.maximum(m, score(t))
            m = jnp.broadcast_to(jnp.max(m, axis=1, keepdims=True), (LANE, LANE))
            l = jnp.zeros((LANE, LANE), jnp.float32)
            row = []
            for t in range(tiles):
                p = jnp.exp2(score(t) - m)
                l = l + p
                row.append(p.astype(jnp.bfloat16))
            plan.append(jnp.concatenate(row, axis=1))
            m = m.T[:1, :]
            l = jnp.sum(l.T, axis=0, keepdims=True)
            copies(out_ref, k, m + jnp.log2(l))
            copies(out_ref, rows // LANE + k, m)
        plan = jnp.concatenate(plan, axis=0)
        total = jnp.dot(plan[:, :half], ya_ref[...], preferred_element_type=jnp.float32)
        total = total + jnp.dot(plan[:, half:], yb_ref[...], preferred_element_type=jnp.float32)
        here = pl.ds(b, BLK)
        held_ref[here, :] = total.astype(jnp.bfloat16)
        copy = pltpu.make_async_copy(held_ref.at[here], p_ref.at[here], sems.at[b // BLK])
        copy.start()
        leaving.append(copy)
    for copy in leaving:
        copy.wait()


def last_kernel(log2a, share, parts_ref, gain_ref, cand_ref, tgt_ref):
    top = share * lax.axis_size(CG) // LANE
    per = LANE // share
    per_xh = top // lax.axis_size("xh")
    mine = lax.axis_index(("xl", "y"))
    lane = lax.broadcasted_iota(jnp.int32, (1, LANE), 1) // share
    lse = merge(parts_ref[:, pl.ds(0, top), :])
    cand_ref[...] = jnp.zeros(cand_ref.shape, jnp.float32)
    row_of = lax.broadcasted_iota(jnp.int32, lse.shape, 0)

    def row(value, at):
        return jnp.sum(jnp.where(row_of == at, value, 0.0), axis=0, keepdims=True)

    def shifted(value, to, at):
        out = jnp.zeros_like(value)
        for off in range(per):
            moved = pltpu.roll(value, ((to - off) % per) * share, 1) if (to - off) % per else value
            out = jnp.where(at == off, moved, out)
        return out

    pieces = jnp.zeros((1, LANE), jnp.float32)
    for h in range(lax.axis_size("xh")):
        value = shifted(row(lse, h * per_xh + mine // per), h, lax.rem(mine, per))
        pieces = jnp.where(lane == h, value, pieces)
    cand_ref[pl.ds(lax.axis_index("z"), 1), :] = (log2a - pieces) / TO2

    me = lax.axis_index(CG)
    own = parts_ref[:, pl.ds(top + me // per, 1), :].reshape(parts_ref.shape[0], LANE)
    gain_ref[...] = shifted(jnp.exp2(own - row(lse, me // per)), 0, lax.rem(me, per))

    n = lax.axis_size(("xl", "y"))
    for k in range(n):
        pair = parts_ref[lax.axis_index("xh") * n + k, pl.ds(2 * top, 2), :]
        tgt_ref[pl.ds(2 * k, 2), :] = pair / TO2


VMEM = pl.BlockSpec(memory_space=pltpu.VMEM)
HBM = pl.BlockSpec(memory_space=pltpu.HBM)


def local(candidates, targets, target_domain, domain_counts):
    f32, bf16 = jnp.float32, jnp.bfloat16
    width = candidates.shape[1]
    plane = lax.axis_size(CG)
    pairs = lax.axis_size(TG)
    depth = lax.axis_size("z")
    share = candidates.shape[0]
    rows = share * plane
    half = targets.shape[0] * depth
    cols = 2 * half
    total_rows = rows * pairs
    total_cols = cols * plane

    def run(kernel, args, outs, scratch=(), special=(), cost=rows * cols):
        special = dict(special)
        return pl.pallas_call(
            kernel,
            in_specs=[special.get(i, VMEM) for i in range(len(args))],
            out_specs=[o[2] if len(o) > 2 else VMEM for o in outs],
            out_shape=[(pltpu.HBM if len(o) > 2 else jax.ShapeDtypeStruct)(o[0], o[1]) for o in outs],
            scratch_shapes=[pltpu.VMEM(*v) if isinstance(v, tuple) else v for v in scratch],
            compiler_params=pltpu.CompilerParams(vmem_limit_bytes=VMEM_LIMIT),
            cost_estimate=pl.CostEstimate(flops=cost * width, bytes_accessed=4 * cost, transcendentals=cost),
        )(*[pltpu.with_memory_space_constraint(a, pltpu.HBM) if special.get(i) is HBM else a for i, a in enumerate(args)])

    def shift(block, by):
        return lax.ppermute(block, "z", [(i, (i + by) % depth) for i in range(depth)])

    (x,) = run(
        spread_kernel,
        (candidates,),
        [((plane, share, width), bf16, HBM)],
        [pltpu.SemaphoreType.DMA((plane,))],
        cost=1,
    )
    x, targets = lax.optimization_barrier((x, targets))
    x = lax.all_to_all(x, CG, 0, 0, tiled=True).reshape(rows, width)
    counts = domain_counts.astype(f32)
    domains = jnp.arange(domain_counts.shape[0], dtype=jnp.int32)
    weight = jnp.sum(jnp.where(target_domain[:, None] == domains[None, :], counts[None, :], 0.0), axis=1)
    logb = jnp.log2(weight / jnp.sum(counts)) + (
        math.log2(domain_counts.shape[0]) - math.log2(total_cols)
    )
    mid = targets.shape[0] // 2
    late, logb = lax.optimization_barrier((targets, logb))
    near = [shift(late, 1), shift(late, -1), shift(targets, 2), shift(targets, -2)]
    far = [shift(near[2], 1), shift(near[3], -1)]
    ends = [shift(far[0][:mid], 1), shift(far[1][mid:], -1)]
    ya = jnp.concatenate([targets] + near + far + ends, axis=0)
    scale = TO2 / width
    ya, x, logb = lax.optimization_barrier((ya, x, logb[None, :]))
    yb = lax.ppermute(ya, "core", [(0, 1), (1, 0)])

    log2a = -math.log2(total_rows)
    row_shape = ((plane, rows // LANE, LANE), f32)
    col_shape = ((pairs, cols // LANE, LANE), f32)
    wide_shape = ((pairs, cols // LANE + 8, LANE), f32)
    last_shape = ((plane, 2 * rows // LANE + 8, LANE), f32)
    stat = ((rows, LANE), f32)
    vec = ((cols // LANE, LANE), f32)
    chalf = ((rows, half), f32)
    ca, m, l, sqx = run(functools.partial(first_cost, scale), (x, ya), [chalf, stat, stat, stat])
    cb, out = run(
        functools.partial(second_cost, scale), (x, sqx, yb, m, l), [chalf, row_shape], [stat, stat]
    )

    def columns(out, shape, *extra):
        parts = lax.all_to_all(out, CG, 0, 0, tiled=True)
        (out,) = run(functools.partial(col_kernel, log2a), (parts, ca, cb, *extra), [shape], [stat])
        return lax.all_to_all(out, TG, 0, 0, tiled=True)

    out, logb = run(
        row_kernel, (columns(out, wide_shape, logb), ca, cb), [row_shape, vec], [vec, vec, stat, stat]
    )
    out, partial = run(
        plan_kernel,
        (columns(out, col_shape), logb, ca, cb, ya, yb),
        [last_shape, ((rows, width), bf16, HBM)],
        [vec, vec, ((rows, width), bf16), pltpu.SemaphoreType.DMA((rows // BLK,))],
    )
    parts = lax.all_to_all(out, CG, 0, 0, tiled=True)
    moved = lax.all_to_all(partial.reshape(plane, share, width), CG, 0, 0, tiled=True)
    gain, cand, tgt = run(
        functools.partial(last_kernel, log2a, share),
        (parts,),
        [((plane, LANE), f32), ((depth, LANE), f32), vec],
    )
    projection = jnp.sum(moved.astype(f32) * gain[:, :share, None], axis=0).astype(bf16)
    for bit in (1, 2, 4):
        cand = cand + lax.ppermute(cand, "z", [(i, i ^ bit) for i in range(depth)])
    return projection, cand.reshape(-1), tgt.reshape(-1)


def solution(mesh):
    fine = Mesh(mesh.devices.reshape(2, -1, 2, mesh.shape["col"] // 2, 2), ROW + COL)
    tgt = P(COL + ROW)
    return jax.shard_map(
        local,
        mesh=fine,
        in_specs=(P(ROW + COL, None), P(COL + ROW, None), tgt, P()),
        out_specs=(P(ROW + COL, None), P(ROW), P(COL)),
        check_vma=False,
    )
```

```python
import functools
import math

import jax
import jax.numpy as jnp
from jax import lax
from jax.experimental import pallas as pl
from jax.experimental.pallas import tpu as pltpu
from jax.sharding import Mesh, PartitionSpec as P

eps = 0.01
LOG2E = math.log2(math.e)
TO2 = LOG2E / eps

ROW = ("xl", "y", "core")
COL = ("z", "xh")
CG = ("xh", "xl", "y")
TG = ("core", "z")
RING = (0, -1, 1, -2, 2, -3, 3, 4)
LANE = 128
SUB = 64
BLK = 256
MIB = 1024 * 1024
VMEM_LIMIT = 30 * MIB


def spread(row):
    return jnp.broadcast_to(row, (LANE, LANE)).T


def fold_lanes(m, l):
    mt, lt = m.T, l.T
    top = jnp.max(mt, axis=0, keepdims=True)
    return top + jnp.log2(jnp.sum(lt * jnp.exp2(mt - top), axis=0, keepdims=True))


def merge(parts):
    top = jnp.max(parts, axis=0)
    return top + jnp.log2(jnp.sum(jnp.exp2(parts - top[None]), axis=0))


def copies(out_ref, at, value):
    for d in range(out_ref.shape[0]):
        out_ref[d, pl.ds(at, 1), :] = value


def spread_kernel(x_ref, out_ref, sems):
    started = []
    for d in range(out_ref.shape[0]):
        copy = pltpu.make_async_copy(x_ref, out_ref.at[d], sems.at[d])
        copy.start()
        started.append(copy)
    for copy in started:
        copy.wait()


def norms(scale, x_ref, out_ref):
    for r in range(0, x_ref.shape[0], LANE):
        acc = jnp.zeros((LANE, LANE), jnp.float32)
        for k in range(0, x_ref.shape[1], LANE):
            x = x_ref[pl.ds(r, LANE), pl.ds(k, LANE)].astype(jnp.float32)
            acc = acc + x * x
        total = jnp.sum(acc, axis=1, keepdims=True) * scale
        out_ref[pl.ds(r, LANE), :] = jnp.broadcast_to(total, (LANE, LANE))


def half_cost(scale, x_ref, sqx_ref, y_ref, c_ref, m_ref, l_ref):
    rows, half = c_ref.shape
    tiles = half // LANE
    sqy = []
    for t in range(tiles):
        acc = jnp.zeros((LANE, LANE), jnp.float32)
        for k in range(0, y_ref.shape[1], LANE):
            y = y_ref[pl.ds(t * LANE, LANE), pl.ds(k, LANE)].astype(jnp.float32)
            acc = acc + y * y
        sqy.append(jnp.sum(acc.T, axis=0, keepdims=True) * scale)
    wide = 512
    for b in range(0, rows, BLK):
        x = x_ref[pl.ds(b, BLK), :]
        for at in range(0, half, wide):
            cross = lax.dot_general(
                x, y_ref[pl.ds(at, wide), :], (((1,), (1,)), ((), ())), preferred_element_type=jnp.float32
            )
            for r in range(0, BLK, SUB):
                here = pl.ds(b + r, SUB)
                sqx = sqx_ref[here, :]
                low = l_ref[here, :] if at else None
                for k in range(wide // LANE):
                    t = at // LANE + k
                    part = cross[r : r + SUB, k * LANE : (k + 1) * LANE]
                    cost = (sqx + sqy[t]) - (2.0 * scale) * part
                    c_ref[here, pl.ds(t * LANE, LANE)] = cost
                    low = cost if low is None else jnp.minimum(low, cost)
                l_ref[here, :] = low
        for r in range(b, b + BLK, SUB):
            here = pl.ds(r, SUB)
            low = l_ref[here, :]
            l = jnp.zeros((SUB, LANE), jnp.float32)
            for t in range(tiles):
                l = l + jnp.exp2(low - c_ref[here, pl.ds(t * LANE, LANE)])
            m_ref[here, :] = -low
            l_ref[here, :] = l


def first_cost(scale, x_ref, y_ref, c_ref, m_ref, l_ref, sqx_ref):
    norms(scale, x_ref, sqx_ref)
    half_cost(scale, x_ref, sqx_ref, y_ref, c_ref, m_ref, l_ref)


def place(tile):
    n = len(RING)
    core = lax.rem(tile // n + lax.axis_index("core"), 2)
    return core * n + lax.rem(lax.axis_index("z") + RING[tile % n] + n, n)


def second_cost(scale, x_ref, sqx_ref, y_ref, m0_ref, l0_ref, c_ref, out_ref, m_ref, l_ref):
    half_cost(scale, x_ref, sqx_ref, y_ref, c_ref, m_ref, l_ref)
    for k in range(c_ref.shape[0] // LANE):
        here = pl.ds(k * LANE, LANE)
        m0, m1 = m0_ref[here, :], m_ref[here, :]
        m = jnp.maximum(m0, m1)
        l = l0_ref[here, :] * jnp.exp2(m0 - m) + l_ref[here, :] * jnp.exp2(m1 - m)
        copies(out_ref, k, fold_lanes(m, l))


def col_kernel(log2a, parts_ref, ca_ref, cb_ref, *refs):
    *logb_ref, out_ref, u_ref = refs
    rows, half = ca_ref.shape
    total = 2 * half // LANE
    if logb_ref:
        copies(out_ref, total, logb_ref[0][...])
        for k in range(total + 1, out_ref.shape[1]):
            copies(out_ref, k, jnp.zeros((1, LANE), jnp.float32))
    u = log2a - merge(parts_ref[...])
    for k in range(rows // LANE):
        u_ref[pl.ds(k * LANE, LANE), :] = spread(u[k : k + 1, :])
    sub, group = 32, 8
    for h, c_ref in enumerate((ca_ref, cb_ref)):
        for k0 in range(0, half // LANE, group):
            ks = range(k0, k0 + group)

            def score(r, k):
                return u_ref[pl.ds(r, sub), :] - c_ref[pl.ds(r, sub), pl.ds(k * LANE, LANE)]

            def top_step(i, m):
                r = pl.multiple_of(i * sub, sub)
                return tuple(jnp.maximum(a, score(r, k)) for a, k in zip(m, ks))

            def sum_step(m, i, l):
                r = pl.multiple_of(i * sub, sub)
                return tuple(a + jnp.exp2(score(r, k) - b) for a, b, k in zip(l, m, ks))

            m = lax.fori_loop(1, rows // sub, top_step, tuple(score(0, k) for k in ks), unroll=4)
            zero = jnp.zeros((sub, LANE), jnp.float32)
            l = lax.fori_loop(
                0, rows // sub, functools.partial(sum_step, m), (zero,) * group, unroll=4
            )
            for a, b, k in zip(l, m, ks):
                top = jnp.max(b, axis=0, keepdims=True)
                e = top + jnp.log2(jnp.sum(a * jnp.exp2(b - top), axis=0, keepdims=True))
                copies(out_ref, place(h * (total // 2) + k), e)


def tgt_pot(parts, logb_ref, v_ref, pot_ref):
    pot_ref[...] = logb_ref[...] - merge(parts)
    for t in range(v_ref.shape[0]):
        v_ref[pl.ds(t, 1), :] = pot_ref[pl.ds(place(t), 1), :]


def scores(v_ref, ca_ref, cb_ref, here):
    tiles = ca_ref.shape[1] // LANE

    def score(t):
        ref = ca_ref if t < tiles else cb_ref
        return v_ref[pl.ds(t, 1), :] - ref[here, pl.ds((t % tiles) * LANE, LANE)]

    return score, 2 * tiles


def row_kernel(parts_ref, ca_ref, cb_ref, out_ref, logb_ref, v_ref, pot_ref, m_ref, l_ref):
    rows = ca_ref.shape[0]
    total = v_ref.shape[0]
    for d in range(total):
        logb_ref[pl.ds(d, 1), :] = parts_ref[d, pl.ds(total, 1), :]
    tgt_pot(parts_ref[:, pl.ds(0, total), :], logb_ref, v_ref, pot_ref)

    def body(i, carry):
        here = pl.ds(pl.multiple_of(i * LANE, LANE), LANE)
        score, tiles = scores(v_ref, ca_ref, cb_ref, here)
        m = score(0)
        for t in range(1, tiles):
            m = jnp.maximum(m, score(t))
        l = jnp.zeros((LANE, LANE), jnp.float32)
        for t in range(tiles):
            l = l + jnp.exp2(score(t) - m)
        m_ref[here, :] = m
        l_ref[here, :] = l
        return carry

    lax.fori_loop(0, rows // LANE, body, 0)
    for k in range(rows // LANE):
        here = pl.ds(k * LANE, LANE)
        copies(out_ref, k, fold_lanes(m_ref[here, :], l_ref[here, :]))


def plan_kernel(parts_ref, logb_ref, ca_ref, cb_ref, ya_ref, yb_ref, out_ref, p_ref, v_ref, pot_ref, held_ref, sems):
    rows, half = ca_ref.shape
    tgt_pot(parts_ref[...], logb_ref, v_ref, pot_ref)
    first = 2 * rows // LANE
    n = pot_ref.shape[0] // 2
    for h in range(2):
        copies(out_ref, first + h, pot_ref[pl.ds(lax.axis_index("z") + h * n, 1), :])
    for k in range(first + 2, out_ref.shape[1]):
        copies(out_ref, k, jnp.zeros((1, LANE), jnp.float32))

    leaving = []
    for b in range(0, rows, BLK):
        plan = []
        for k in range(b // LANE, (b + BLK) // LANE):
            score, tiles = scores(v_ref, ca_ref, cb_ref, pl.ds(k * LANE, LANE))
            m = score(0)
            for t in range(1, tiles):
                m = jnp.maximum(m, score(t))
            m = jnp.broadcast_to(jnp.max(m, axis=1, keepdims=True), (LANE, LANE))
            l = jnp.zeros((LANE, LANE), jnp.float32)
            row = []
            for t in range(tiles):
                p = jnp.exp2(score(t) - m)
                l = l + p
                row.append(p.astype(jnp.bfloat16))
            plan.append(jnp.concatenate(row, axis=1))
            m = m.T[:1, :]
            l = jnp.sum(l.T, axis=0, keepdims=True)
            copies(out_ref, k, m + jnp.log2(l))
            copies(out_ref, rows // LANE + k, m)
        plan = jnp.concatenate(plan, axis=0)
        total = jnp.dot(plan[:, :half], ya_ref[...], preferred_element_type=jnp.float32)
        total = total + jnp.dot(plan[:, half:], yb_ref[...], preferred_element_type=jnp.float32)
        here = pl.ds(b, BLK)
        held_ref[here, :] = total.astype(jnp.bfloat16)
        copy = pltpu.make_async_copy(held_ref.at[here], p_ref.at[here], sems.at[b // BLK])
        copy.start()
        leaving.append(copy)
    for copy in leaving:
        copy.wait()


def last_kernel(log2a, share, parts_ref, gain_ref, cand_ref, tgt_ref):
    top = share * lax.axis_size(CG) // LANE
    per = LANE // share
    per_xh = top // lax.axis_size("xh")
    mine = lax.axis_index(("xl", "y"))
    lane = lax.broadcasted_iota(jnp.int32, (1, LANE), 1) // share
    lse = merge(parts_ref[:, pl.ds(0, top), :])
    cand_ref[...] = jnp.zeros(cand_ref.shape, jnp.float32)
    row_of = lax.broadcasted_iota(jnp.int32, lse.shape, 0)

    def row(value, at):
        return jnp.sum(jnp.where(row_of == at, value, 0.0), axis=0, keepdims=True)

    def shifted(value, to, at):
        out = jnp.zeros_like(value)
        for off in range(per):
            moved = pltpu.roll(value, ((to - off) % per) * share, 1) if (to - off) % per else value
            out = jnp.where(at == off, moved, out)
        return out

    pieces = jnp.zeros((1, LANE), jnp.float32)
    for h in range(lax.axis_size("xh")):
        value = shifted(row(lse, h * per_xh + mine // per), h, lax.rem(mine, per))
        pieces = jnp.where(lane == h, value, pieces)
    cand_ref[pl.ds(lax.axis_index("z"), 1), :] = (log2a - pieces) / TO2

    me = lax.axis_index(CG)
    own = parts_ref[:, pl.ds(top + me // per, 1), :].reshape(parts_ref.shape[0], LANE)
    gain_ref[...] = shifted(jnp.exp2(own - row(lse, me // per)), 0, lax.rem(me, per))

    n = lax.axis_size(("xl", "y"))
    for k in range(n):
        pair = parts_ref[lax.axis_index("xh") * n + k, pl.ds(2 * top, 2), :]
        tgt_ref[pl.ds(2 * k, 2), :] = pair / TO2


VMEM = pl.BlockSpec(memory_space=pltpu.VMEM)
HBM = pl.BlockSpec(memory_space=pltpu.HBM)


def local(candidates, targets, target_domain, domain_counts):
    f32, bf16 = jnp.float32, jnp.bfloat16
    width = candidates.shape[1]
    plane = lax.axis_size(CG)
    pairs = lax.axis_size(TG)
    depth = lax.axis_size("z")
    share = candidates.shape[0]
    rows = share * plane
    half = targets.shape[0] * depth
    cols = 2 * half
    total_rows = rows * pairs
    total_cols = cols * plane

    def run(kernel, args, outs, scratch=(), special=(), cost=rows * cols):
        special = dict(special)
        return pl.pallas_call(
            kernel,
            in_specs=[special.get(i, VMEM) for i in range(len(args))],
            out_specs=[o[2] if len(o) > 2 else VMEM for o in outs],
            out_shape=[(pltpu.HBM if len(o) > 2 else jax.ShapeDtypeStruct)(o[0], o[1]) for o in outs],
            scratch_shapes=[pltpu.VMEM(*v) if isinstance(v, tuple) else v for v in scratch],
            compiler_params=pltpu.CompilerParams(vmem_limit_bytes=VMEM_LIMIT),
            cost_estimate=pl.CostEstimate(flops=cost * width, bytes_accessed=4 * cost, transcendentals=cost),
        )(*[pltpu.with_memory_space_constraint(a, pltpu.HBM) if special.get(i) is HBM else a for i, a in enumerate(args)])

    def shift(block, by):
        return lax.ppermute(block, "z", [(i, (i + by) % depth) for i in range(depth)])

    (x,) = run(
        spread_kernel,
        (candidates,),
        [((plane, share, width), bf16, HBM)],
        [pltpu.SemaphoreType.DMA((plane,))],
        cost=1,
    )
    x, targets = lax.optimization_barrier((x, targets))
    x = lax.all_to_all(x, CG, 0, 0, tiled=True).reshape(rows, width)
    counts = domain_counts.astype(f32)
    domains = jnp.arange(domain_counts.shape[0], dtype=jnp.int32)
    weight = jnp.sum(jnp.where(target_domain[:, None] == domains[None, :], counts[None, :], 0.0), axis=1)
    logb = jnp.log2(weight / jnp.sum(counts)) + (
        math.log2(domain_counts.shape[0]) - math.log2(total_cols)
    )
    mid = targets.shape[0] // 2
    late, logb = lax.optimization_barrier((targets, logb))
    near = [shift(late, 1), shift(late, -1), shift(targets, 2), shift(targets, -2)]
    far = [shift(near[2], 1), shift(near[3], -1)]
    ends = [shift(far[0][:mid], 1), shift(far[1][mid:], -1)]
    ya = jnp.concatenate([targets] + near + far + ends, axis=0)
    scale = TO2 / width
    ya, x, logb = lax.optimization_barrier((ya, x, logb[None, :]))
    yb = lax.ppermute(ya, "core", [(0, 1), (1, 0)])

    log2a = -math.log2(total_rows)
    row_shape = ((plane, rows // LANE, LANE), f32)
    col_shape = ((pairs, cols // LANE, LANE), f32)
    wide_shape = ((pairs, cols // LANE + 8, LANE), f32)
    last_shape = ((plane, 2 * rows // LANE + 8, LANE), f32)
    stat = ((rows, LANE), f32)
    vec = ((cols // LANE, LANE), f32)
    chalf = ((rows, half), f32)
    ca, m, l, sqx = run(functools.partial(first_cost, scale), (x, ya), [chalf, stat, stat, stat])
    cb, out = run(
        functools.partial(second_cost, scale), (x, sqx, yb, m, l), [chalf, row_shape], [stat, stat]
    )

    def columns(out, shape, *extra):
        parts = lax.all_to_all(out, CG, 0, 0, tiled=True)
        (out,) = run(functools.partial(col_kernel, log2a), (parts, ca, cb, *extra), [shape], [stat])
        return lax.all_to_all(out, TG, 0, 0, tiled=True)

    out, logb = run(
        row_kernel, (columns(out, wide_shape, logb), ca, cb), [row_shape, vec], [vec, vec, stat, stat]
    )
    out, partial = run(
        plan_kernel,
        (columns(out, col_shape), logb, ca, cb, ya, yb),
        [last_shape, ((rows, width), bf16, HBM)],
        [vec, vec, ((rows, width), bf16), pltpu.SemaphoreType.DMA((rows // BLK,))],
    )
    parts = lax.all_to_all(out, CG, 0, 0, tiled=True)
    moved = lax.all_to_all(partial.reshape(plane, share, width), CG, 0, 0, tiled=True)
    gain, cand, tgt = run(
        functools.partial(last_kernel, log2a, share),
        (parts,),
        [((plane, LANE), f32), ((depth, LANE), f32), vec],
    )
    projection = jnp.sum(moved.astype(f32) * gain[:, :share, None], axis=0).astype(bf16)
    for bit in (1, 2, 4):
        cand = cand + lax.ppermute(cand, "z", [(i, i ^ bit) for i in range(depth)])
    return projection, cand.reshape(-1), tgt.reshape(-1)


def solution(mesh):
    fine = Mesh(mesh.devices.reshape(2, -1, 2, mesh.shape["col"] // 2, 2), ROW + COL)
    tgt = P(COL + ROW)
    return jax.shard_map(
        local,
        mesh=fine,
        in_specs=(P(ROW + COL, None), P(COL + ROW, None), tgt, P()),
        out_specs=(P(ROW + COL, None), P(ROW), P(COL)),
        check_vma=False,
    )
```

```python
import functools
import math

import jax
import jax.numpy as jnp
from jax import lax
from jax.experimental import pallas as pl
from jax.experimental.pallas import tpu as pltpu
from jax.sharding import Mesh, PartitionSpec as P

eps = 0.01
LOG2E = math.log2(math.e)
TO2 = LOG2E / eps

ROW = ("xl", "y", "core")
COL = ("z", "xh")
CG = ("xh", "xl", "y")
TG = ("core", "z")
RING = (0, -1, 1, -2, 2, -3, 3, 4)
LANE = 128
SUB = 64
BLK = 256
MIB = 1024 * 1024
VMEM_LIMIT = 30 * MIB


def spread(row):
    return jnp.broadcast_to(row, (LANE, LANE)).T


def fold_lanes(m, l):
    mt, lt = m.T, l.T
    top = jnp.max(mt, axis=0, keepdims=True)
    return top + jnp.log2(jnp.sum(lt * jnp.exp2(mt - top), axis=0, keepdims=True))


def merge(parts):
    top = jnp.max(parts, axis=0)
    return top + jnp.log2(jnp.sum(jnp.exp2(parts - top[None]), axis=0))


def copies(out_ref, at, value):
    for d in range(out_ref.shape[0]):
        out_ref[d, pl.ds(at, 1), :] = value


def spread_kernel(x_ref, out_ref, sems):
    started = []
    for d in range(out_ref.shape[0]):
        copy = pltpu.make_async_copy(x_ref, out_ref.at[d], sems.at[d])
        copy.start()
        started.append(copy)
    for copy in started:
        copy.wait()


def norms(scale, x_ref, out_ref):
    for r in range(0, x_ref.shape[0], LANE):
        acc = jnp.zeros((LANE, LANE), jnp.float32)
        for k in range(0, x_ref.shape[1], LANE):
            x = x_ref[pl.ds(r, LANE), pl.ds(k, LANE)].astype(jnp.float32)
            acc = acc + x * x
        total = jnp.sum(acc, axis=1, keepdims=True) * scale
        out_ref[pl.ds(r, LANE), :] = jnp.broadcast_to(total, (LANE, LANE))


def half_cost(scale, x_ref, sqx_ref, y_ref, c_ref, m_ref, l_ref):
    rows, half = c_ref.shape
    tiles = half // LANE
    sqy = []
    for t in range(tiles):
        acc = jnp.zeros((LANE, LANE), jnp.float32)
        for k in range(0, y_ref.shape[1], LANE):
            y = y_ref[pl.ds(t * LANE, LANE), pl.ds(k, LANE)].astype(jnp.float32)
            acc = acc + y * y
        sqy.append(jnp.sum(acc.T, axis=0, keepdims=True) * scale)
    wide = 512
    for b in range(0, rows, BLK):
        x = x_ref[pl.ds(b, BLK), :]
        for at in range(0, half, wide):
            cross = lax.dot_general(
                x, y_ref[pl.ds(at, wide), :], (((1,), (1,)), ((), ())), preferred_element_type=jnp.float32
            )
            for r in range(0, BLK, SUB):
                here = pl.ds(b + r, SUB)
                sqx = sqx_ref[here, :]
                low = l_ref[here, :] if at else None
                for k in range(wide // LANE):
                    t = at // LANE + k
                    part = cross[r : r + SUB, k * LANE : (k + 1) * LANE]
                    cost = (sqx + sqy[t]) - (2.0 * scale) * part
                    c_ref[here, pl.ds(t * LANE, LANE)] = cost
                    low = cost if low is None else jnp.minimum(low, cost)
                l_ref[here, :] = low
        for r in range(b, b + BLK, SUB):
            here = pl.ds(r, SUB)
            low = l_ref[here, :]
            l = jnp.zeros((SUB, LANE), jnp.float32)
            for t in range(tiles):
                l = l + jnp.exp2(low - c_ref[here, pl.ds(t * LANE, LANE)])
            m_ref[here, :] = -low
            l_ref[here, :] = l


def first_cost(scale, x_ref, y_ref, c_ref, m_ref, l_ref, sqx_ref):
    norms(scale, x_ref, sqx_ref)
    half_cost(scale, x_ref, sqx_ref, y_ref, c_ref, m_ref, l_ref)


def place(tile):
    n = len(RING)
    core = lax.rem(tile // n + lax.axis_index("core"), 2)
    return core * n + lax.rem(lax.axis_index("z") + RING[tile % n] + n, n)


def second_cost(scale, x_ref, sqx_ref, y_ref, m0_ref, l0_ref, c_ref, out_ref, m_ref, l_ref):
    half_cost(scale, x_ref, sqx_ref, y_ref, c_ref, m_ref, l_ref)
    for k in range(c_ref.shape[0] // LANE):
        here = pl.ds(k * LANE, LANE)
        m0, m1 = m0_ref[here, :], m_ref[here, :]
        m = jnp.maximum(m0, m1)
        l = l0_ref[here, :] * jnp.exp2(m0 - m) + l_ref[here, :] * jnp.exp2(m1 - m)
        copies(out_ref, k, fold_lanes(m, l))


def col_kernel(log2a, parts_ref, ca_ref, cb_ref, *refs):
    *logb_ref, out_ref, u_ref = refs
    rows, half = ca_ref.shape
    total = 2 * half // LANE
    if logb_ref:
        copies(out_ref, total, logb_ref[0][...])
        for k in range(total + 1, out_ref.shape[1]):
            copies(out_ref, k, jnp.zeros((1, LANE), jnp.float32))
    u = log2a - merge(parts_ref[...])
    for k in range(rows // LANE):
        u_ref[pl.ds(k * LANE, LANE), :] = spread(u[k : k + 1, :])
    sub, group = 32, 8
    for h, c_ref in enumerate((ca_ref, cb_ref)):
        for k0 in range(0, half // LANE, group):
            ks = range(k0, k0 + group)

            def score(r, k):
                return u_ref[pl.ds(r, sub), :] - c_ref[pl.ds(r, sub), pl.ds(k * LANE, LANE)]

            def top_step(i, m):
                r = pl.multiple_of(i * sub, sub)
                return tuple(jnp.maximum(a, score(r, k)) for a, k in zip(m, ks))

            def sum_step(m, i, l):
                r = pl.multiple_of(i * sub, sub)
                return tuple(a + jnp.exp2(score(r, k) - b) for a, b, k in zip(l, m, ks))

            m = lax.fori_loop(1, rows // sub, top_step, tuple(score(0, k) for k in ks), unroll=4)
            zero = jnp.zeros((sub, LANE), jnp.float32)
            l = lax.fori_loop(
                0, rows // sub, functools.partial(sum_step, m), (zero,) * group, unroll=4
            )
            for a, b, k in zip(l, m, ks):
                top = jnp.max(b, axis=0, keepdims=True)
                e = top + jnp.log2(jnp.sum(a * jnp.exp2(b - top), axis=0, keepdims=True))
                copies(out_ref, place(h * (total // 2) + k), e)


def tgt_pot(parts, logb_ref, v_ref, pot_ref):
    pot_ref[...] = logb_ref[...] - merge(parts)
    for t in range(v_ref.shape[0]):
        v_ref[pl.ds(t, 1), :] = pot_ref[pl.ds(place(t), 1), :]


def scores(v_ref, ca_ref, cb_ref, here):
    tiles = ca_ref.shape[1] // LANE

    def score(t):
        ref = ca_ref if t < tiles else cb_ref
        return v_ref[pl.ds(t, 1), :] - ref[here, pl.ds((t % tiles) * LANE, LANE)]

    return score, 2 * tiles


def row_kernel(parts_ref, ca_ref, cb_ref, out_ref, logb_ref, v_ref, pot_ref, m_ref, l_ref):
    rows = ca_ref.shape[0]
    total = v_ref.shape[0]
    for d in range(total):
        logb_ref[pl.ds(d, 1), :] = parts_ref[d, pl.ds(total, 1), :]
    tgt_pot(parts_ref[:, pl.ds(0, total), :], logb_ref, v_ref, pot_ref)

    def body(i, carry):
        here = pl.ds(pl.multiple_of(i * LANE, LANE), LANE)
        score, tiles = scores(v_ref, ca_ref, cb_ref, here)
        m = score(0)
        for t in range(1, tiles):
            m = jnp.maximum(m, score(t))
        l = jnp.zeros((LANE, LANE), jnp.float32)
        for t in range(tiles):
            l = l + jnp.exp2(score(t) - m)
        m_ref[here, :] = m
        l_ref[here, :] = l
        return carry

    lax.fori_loop(0, rows // LANE, body, 0)
    for k in range(rows // LANE):
        here = pl.ds(k * LANE, LANE)
        copies(out_ref, k, fold_lanes(m_ref[here, :], l_ref[here, :]))


def plan_kernel(parts_ref, logb_ref, ca_ref, cb_ref, ya_ref, yb_ref, out_ref, p_ref, v_ref, pot_ref, held_ref, sems):
    rows, half = ca_ref.shape
    tgt_pot(parts_ref[...], logb_ref, v_ref, pot_ref)
    first = 2 * rows // LANE
    n = pot_ref.shape[0] // 2
    for h in range(2):
        copies(out_ref, first + h, pot_ref[pl.ds(lax.axis_index("z") + h * n, 1), :])
    for k in range(first + 2, out_ref.shape[1]):
        copies(out_ref, k, jnp.zeros((1, LANE), jnp.float32))

    leaving = []
    for b in range(0, rows, BLK):
        plan = []
        for k in range(b // LANE, (b + BLK) // LANE):
            score, tiles = scores(v_ref, ca_ref, cb_ref, pl.ds(k * LANE, LANE))
            m = score(0)
            for t in range(1, tiles):
                m = jnp.maximum(m, score(t))
            m = jnp.broadcast_to(jnp.max(m, axis=1, keepdims=True), (LANE, LANE))
            l = jnp.zeros((LANE, LANE), jnp.float32)
            row = []
            for t in range(tiles):
                p = jnp.exp2(score(t) - m)
                l = l + p
                row.append(p.astype(jnp.bfloat16))
            plan.append(jnp.concatenate(row, axis=1))
            m = m.T[:1, :]
            l = jnp.sum(l.T, axis=0, keepdims=True)
            copies(out_ref, k, m + jnp.log2(l))
            copies(out_ref, rows // LANE + k, m)
        plan = jnp.concatenate(plan, axis=0)
        total = jnp.dot(plan[:, :half], ya_ref[...], preferred_element_type=jnp.float32)
        total = total + jnp.dot(plan[:, half:], yb_ref[...], preferred_element_type=jnp.float32)
        here = pl.ds(b, BLK)
        held_ref[here, :] = total.astype(jnp.bfloat16)
        copy = pltpu.make_async_copy(held_ref.at[here], p_ref.at[here], sems.at[b // BLK])
        copy.start()
        leaving.append(copy)
    for copy in leaving:
        copy.wait()


def last_kernel(log2a, share, parts_ref, gain_ref, cand_ref, tgt_ref):
    top = share * lax.axis_size(CG) // LANE
    per = LANE // share
    per_xh = top // lax.axis_size("xh")
    mine = lax.axis_index(("xl", "y"))
    lane = lax.broadcasted_iota(jnp.int32, (1, LANE), 1) // share
    lse = merge(parts_ref[:, pl.ds(0, top), :])
    cand_ref[...] = jnp.zeros(cand_ref.shape, jnp.float32)
    row_of = lax.broadcasted_iota(jnp.int32, lse.shape, 0)

    def row(value, at):
        return jnp.sum(jnp.where(row_of == at, value, 0.0), axis=0, keepdims=True)

    def shifted(value, to, at):
        out = jnp.zeros_like(value)
        for off in range(per):
            moved = pltpu.roll(value, ((to - off) % per) * share, 1) if (to - off) % per else value
            out = jnp.where(at == off, moved, out)
        return out

    pieces = jnp.zeros((1, LANE), jnp.float32)
    for h in range(lax.axis_size("xh")):
        value = shifted(row(lse, h * per_xh + mine // per), h, lax.rem(mine, per))
        pieces = jnp.where(lane == h, value, pieces)
    cand_ref[pl.ds(lax.axis_index("z"), 1), :] = (log2a - pieces) / TO2

    me = lax.axis_index(CG)
    own = parts_ref[:, pl.ds(top + me // per, 1), :].reshape(parts_ref.shape[0], LANE)
    gain_ref[...] = shifted(jnp.exp2(own - row(lse, me // per)), 0, lax.rem(me, per))

    n = lax.axis_size(("xl", "y"))
    for k in range(n):
        pair = parts_ref[lax.axis_index("xh") * n + k, pl.ds(2 * top, 2), :]
        tgt_ref[pl.ds(2 * k, 2), :] = pair / TO2


VMEM = pl.BlockSpec(memory_space=pltpu.VMEM)
HBM = pl.BlockSpec(memory_space=pltpu.HBM)


def local(candidates, targets, target_domain, domain_counts):
    f32, bf16 = jnp.float32, jnp.bfloat16
    width = candidates.shape[1]
    plane = lax.axis_size(CG)
    pairs = lax.axis_size(TG)
    depth = lax.axis_size("z")
    share = candidates.shape[0]
    rows = share * plane
    half = targets.shape[0] * depth
    cols = 2 * half
    total_rows = rows * pairs
    total_cols = cols * plane

    def run(kernel, args, outs, scratch=(), special=(), cost=rows * cols):
        special = dict(special)
        return pl.pallas_call(
            kernel,
            in_specs=[special.get(i, VMEM) for i in range(len(args))],
            out_specs=[o[2] if len(o) > 2 else VMEM for o in outs],
            out_shape=[(pltpu.HBM if len(o) > 2 else jax.ShapeDtypeStruct)(o[0], o[1]) for o in outs],
            scratch_shapes=[pltpu.VMEM(*v) if isinstance(v, tuple) else v for v in scratch],
            compiler_params=pltpu.CompilerParams(vmem_limit_bytes=VMEM_LIMIT),
            cost_estimate=pl.CostEstimate(flops=cost * width, bytes_accessed=4 * cost, transcendentals=cost),
        )(*[pltpu.with_memory_space_constraint(a, pltpu.HBM) if special.get(i) is HBM else a for i, a in enumerate(args)])

    def shift(block, by):
        return lax.ppermute(block, "z", [(i, (i + by) % depth) for i in range(depth)])

    (x,) = run(
        spread_kernel,
        (candidates,),
        [((plane, share, width), bf16, HBM)],
        [pltpu.SemaphoreType.DMA((plane,))],
        cost=1,
    )
    x, targets = lax.optimization_barrier((x, targets))
    x = lax.all_to_all(x, CG, 0, 0, tiled=True).reshape(rows, width)
    counts = domain_counts.astype(f32)
    domains = jnp.arange(domain_counts.shape[0], dtype=jnp.int32)
    weight = jnp.sum(jnp.where(target_domain[:, None] == domains[None, :], counts[None, :], 0.0), axis=1)
    logb = jnp.log2(weight / jnp.sum(counts)) + (
        math.log2(domain_counts.shape[0]) - math.log2(total_cols)
    )
    mid = targets.shape[0] // 2
    two = [shift(targets, 2), shift(targets, -2)]
    far = [shift(two[0], 1), shift(two[1], -1)]
    late, *far = lax.optimization_barrier((targets, *far))
    near = [shift(late, 1), shift(late, -1)] + two
    ends = [shift(far[0][:mid], 1), shift(far[1][mid:], -1)]
    ya = jnp.concatenate([targets] + near + far + ends, axis=0)
    scale = TO2 / width
    ya, x, logb = lax.optimization_barrier((ya, x, logb[None, :]))
    yb = lax.ppermute(ya, "core", [(0, 1), (1, 0)])

    log2a = -math.log2(total_rows)
    row_shape = ((plane, rows // LANE, LANE), f32)
    col_shape = ((pairs, cols // LANE, LANE), f32)
    wide_shape = ((pairs, cols // LANE + 8, LANE), f32)
    last_shape = ((plane, 2 * rows // LANE + 8, LANE), f32)
    stat = ((rows, LANE), f32)
    vec = ((cols // LANE, LANE), f32)
    chalf = ((rows, half), f32)
    ca, m, l, sqx = run(functools.partial(first_cost, scale), (x, ya), [chalf, stat, stat, stat])
    cb, out = run(
        functools.partial(second_cost, scale), (x, sqx, yb, m, l), [chalf, row_shape], [stat, stat]
    )

    def columns(out, shape, *extra):
        parts = lax.all_to_all(out, CG, 0, 0, tiled=True)
        (out,) = run(functools.partial(col_kernel, log2a), (parts, ca, cb, *extra), [shape], [stat])
        return lax.all_to_all(out, TG, 0, 0, tiled=True)

    out, logb = run(
        row_kernel, (columns(out, wide_shape, logb), ca, cb), [row_shape, vec], [vec, vec, stat, stat]
    )
    out, partial = run(
        plan_kernel,
        (columns(out, col_shape), logb, ca, cb, ya, yb),
        [last_shape, ((rows, width), bf16, HBM)],
        [vec, vec, ((rows, width), bf16), pltpu.SemaphoreType.DMA((rows // BLK,))],
    )
    parts = lax.all_to_all(out, CG, 0, 0, tiled=True)
    moved = lax.all_to_all(partial.reshape(plane, share, width), CG, 0, 0, tiled=True)
    gain, cand, tgt = run(
        functools.partial(last_kernel, log2a, share),
        (parts,),
        [((plane, LANE), f32), ((depth, LANE), f32), vec],
    )
    projection = jnp.sum(moved.astype(f32) * gain[:, :share, None], axis=0).astype(bf16)
    for bit in (1, 2, 4):
        cand = cand + lax.ppermute(cand, "z", [(i, i ^ bit) for i in range(depth)])
    return projection, cand.reshape(-1), tgt.reshape(-1)


def solution(mesh):
    fine = Mesh(mesh.devices.reshape(2, -1, 2, mesh.shape["col"] // 2, 2), ROW + COL)
    tgt = P(COL + ROW)
    return jax.shard_map(
        local,
        mesh=fine,
        in_specs=(P(ROW + COL, None), P(COL + ROW, None), tgt, P()),
        out_specs=(P(ROW + COL, None), P(ROW), P(COL)),
        check_vma=False,
    )
```

```python
import functools
import math

import jax
import jax.numpy as jnp
from jax import lax
from jax.experimental import pallas as pl
from jax.experimental.pallas import tpu as pltpu
from jax.sharding import Mesh, PartitionSpec as P

eps = 0.01
LOG2E = math.log2(math.e)
TO2 = LOG2E / eps

ROW = ("xl", "y", "core")
COL = ("z", "xh")
CG = ("xh", "xl", "y")
TG = ("core", "z")
RING = (0, -1, 1, -2, 2, -3, 3, 4)
LANE = 128
SUB = 64
BLK = 256
MIB = 1024 * 1024
VMEM_LIMIT = 30 * MIB


def spread(row):
    return jnp.broadcast_to(row, (LANE, LANE)).T


def fold_lanes(m, l):
    mt, lt = m.T, l.T
    top = jnp.max(mt, axis=0, keepdims=True)
    return top + jnp.log2(jnp.sum(lt * jnp.exp2(mt - top), axis=0, keepdims=True))


def merge(parts):
    top = jnp.max(parts, axis=0)
    return top + jnp.log2(jnp.sum(jnp.exp2(parts - top[None]), axis=0))


def copies(out_ref, at, value):
    for d in range(out_ref.shape[0]):
        out_ref[d, pl.ds(at, 1), :] = value


def spread_kernel(x_ref, out_ref, sems):
    started = []
    for d in range(out_ref.shape[0]):
        copy = pltpu.make_async_copy(x_ref, out_ref.at[d], sems.at[d])
        copy.start()
        started.append(copy)
    for copy in started:
        copy.wait()


def norms(scale, x_ref, out_ref):
    for r in range(0, x_ref.shape[0], LANE):
        acc = jnp.zeros((LANE, LANE), jnp.float32)
        for k in range(0, x_ref.shape[1], LANE):
            x = x_ref[pl.ds(r, LANE), pl.ds(k, LANE)].astype(jnp.float32)
            acc = acc + x * x
        total = jnp.sum(acc, axis=1, keepdims=True) * scale
        out_ref[pl.ds(r, LANE), :] = jnp.broadcast_to(total, (LANE, LANE))


def half_cost(scale, x_ref, sqx_ref, y_ref, c_ref, m_ref, l_ref):
    rows, half = c_ref.shape
    tiles = half // LANE
    sqy = []
    for t in range(tiles):
        acc = jnp.zeros((LANE, LANE), jnp.float32)
        for k in range(0, y_ref.shape[1], LANE):
            y = y_ref[pl.ds(t * LANE, LANE), pl.ds(k, LANE)].astype(jnp.float32)
            acc = acc + y * y
        sqy.append(jnp.sum(acc.T, axis=0, keepdims=True) * scale)
    wide = 512
    for b in range(0, rows, BLK):
        x = x_ref[pl.ds(b, BLK), :]
        for at in range(0, half, wide):
            cross = lax.dot_general(
                x, y_ref[pl.ds(at, wide), :], (((1,), (1,)), ((), ())), preferred_element_type=jnp.float32
            )
            for r in range(0, BLK, SUB):
                here = pl.ds(b + r, SUB)
                sqx = sqx_ref[here, :]
                low = l_ref[here, :] if at else None
                for k in range(wide // LANE):
                    t = at // LANE + k
                    part = cross[r : r + SUB, k * LANE : (k + 1) * LANE]
                    cost = (sqx + sqy[t]) - (2.0 * scale) * part
                    c_ref[here, pl.ds(t * LANE, LANE)] = cost
                    low = cost if low is None else jnp.minimum(low, cost)
                l_ref[here, :] = low
        for r in range(b, b + BLK, SUB):
            here = pl.ds(r, SUB)
            low = l_ref[here, :]
            l = jnp.zeros((SUB, LANE), jnp.float32)
            for t in range(tiles):
                l = l + jnp.exp2(low - c_ref[here, pl.ds(t * LANE, LANE)])
            m_ref[here, :] = -low
            l_ref[here, :] = l


def first_cost(scale, x_ref, y_ref, c_ref, m_ref, l_ref, sqx_ref):
    norms(scale, x_ref, sqx_ref)
    half_cost(scale, x_ref, sqx_ref, y_ref, c_ref, m_ref, l_ref)


def place(tile):
    n = len(RING)
    core = lax.rem(tile // n + lax.axis_index("core"), 2)
    return core * n + lax.rem(lax.axis_index("z") + RING[tile % n] + n, n)


def second_cost(scale, x_ref, sqx_ref, y_ref, m0_ref, l0_ref, c_ref, out_ref, m_ref, l_ref):
    half_cost(scale, x_ref, sqx_ref, y_ref, c_ref, m_ref, l_ref)
    for k in range(c_ref.shape[0] // LANE):
        here = pl.ds(k * LANE, LANE)
        m0, m1 = m0_ref[here, :], m_ref[here, :]
        m = jnp.maximum(m0, m1)
        l = l0_ref[here, :] * jnp.exp2(m0 - m) + l_ref[here, :] * jnp.exp2(m1 - m)
        copies(out_ref, k, fold_lanes(m, l))


def col_kernel(log2a, parts_ref, ca_ref, cb_ref, *refs):
    *logb_ref, out_ref, u_ref = refs
    rows, half = ca_ref.shape
    total = 2 * half // LANE
    if logb_ref:
        copies(out_ref, total, logb_ref[0][...])
        for k in range(total + 1, out_ref.shape[1]):
            copies(out_ref, k, jnp.zeros((1, LANE), jnp.float32))
    u = log2a - merge(parts_ref[...])
    for k in range(rows // LANE):
        u_ref[pl.ds(k * LANE, LANE), :] = spread(u[k : k + 1, :])
    sub, group = 32, 8
    for h, c_ref in enumerate((ca_ref, cb_ref)):
        for k0 in range(0, half // LANE, group):
            ks = range(k0, k0 + group)

            def score(r, k):
                return u_ref[pl.ds(r, sub), :] - c_ref[pl.ds(r, sub), pl.ds(k * LANE, LANE)]

            def top_step(i, m):
                r = pl.multiple_of(i * sub, sub)
                return tuple(jnp.maximum(a, score(r, k)) for a, k in zip(m, ks))

            def sum_step(m, i, l):
                r = pl.multiple_of(i * sub, sub)
                return tuple(a + jnp.exp2(score(r, k) - b) for a, b, k in zip(l, m, ks))

            m = lax.fori_loop(1, rows // sub, top_step, tuple(score(0, k) for k in ks), unroll=8)
            zero = jnp.zeros((sub, LANE), jnp.float32)
            l = lax.fori_loop(
                0, rows // sub, functools.partial(sum_step, m), (zero,) * group, unroll=8
            )
            for a, b, k in zip(l, m, ks):
                top = jnp.max(b, axis=0, keepdims=True)
                e = top + jnp.log2(jnp.sum(a * jnp.exp2(b - top), axis=0, keepdims=True))
                copies(out_ref, place(h * (total // 2) + k), e)


def tgt_pot(parts, logb_ref, v_ref, pot_ref):
    pot_ref[...] = logb_ref[...] - merge(parts)
    for t in range(v_ref.shape[0]):
        v_ref[pl.ds(t, 1), :] = pot_ref[pl.ds(place(t), 1), :]


def scores(v_ref, ca_ref, cb_ref, here):
    tiles = ca_ref.shape[1] // LANE

    def score(t):
        ref = ca_ref if t < tiles else cb_ref
        return v_ref[pl.ds(t, 1), :] - ref[here, pl.ds((t % tiles) * LANE, LANE)]

    return score, 2 * tiles


def row_kernel(parts_ref, ca_ref, cb_ref, out_ref, logb_ref, v_ref, pot_ref, m_ref, l_ref):
    rows = ca_ref.shape[0]
    total = v_ref.shape[0]
    for d in range(total):
        logb_ref[pl.ds(d, 1), :] = parts_ref[d, pl.ds(total, 1), :]
    tgt_pot(parts_ref[:, pl.ds(0, total), :], logb_ref, v_ref, pot_ref)

    def body(i, carry):
        here = pl.ds(pl.multiple_of(i * LANE, LANE), LANE)
        score, tiles = scores(v_ref, ca_ref, cb_ref, here)
        m = score(0)
        for t in range(1, tiles):
            m = jnp.maximum(m, score(t))
        l = jnp.zeros((LANE, LANE), jnp.float32)
        for t in range(tiles):
            l = l + jnp.exp2(score(t) - m)
        m_ref[here, :] = m
        l_ref[here, :] = l
        return carry

    lax.fori_loop(0, rows // LANE, body, 0)
    for k in range(rows // LANE):
        here = pl.ds(k * LANE, LANE)
        copies(out_ref, k, fold_lanes(m_ref[here, :], l_ref[here, :]))


def plan_kernel(parts_ref, logb_ref, ca_ref, cb_ref, ya_ref, yb_ref, out_ref, p_ref, v_ref, pot_ref, held_ref, sems):
    rows, half = ca_ref.shape
    tgt_pot(parts_ref[...], logb_ref, v_ref, pot_ref)
    first = 2 * rows // LANE
    n = pot_ref.shape[0] // 2
    for h in range(2):
        copies(out_ref, first + h, pot_ref[pl.ds(lax.axis_index("z") + h * n, 1), :])
    for k in range(first + 2, out_ref.shape[1]):
        copies(out_ref, k, jnp.zeros((1, LANE), jnp.float32))

    leaving = []
    for b in range(0, rows, BLK):
        plan = []
        for k in range(b // LANE, (b + BLK) // LANE):
            score, tiles = scores(v_ref, ca_ref, cb_ref, pl.ds(k * LANE, LANE))
            m = score(0)
            for t in range(1, tiles):
                m = jnp.maximum(m, score(t))
            m = jnp.broadcast_to(jnp.max(m, axis=1, keepdims=True), (LANE, LANE))
            l = jnp.zeros((LANE, LANE), jnp.float32)
            row = []
            for t in range(tiles):
                p = jnp.exp2(score(t) - m)
                l = l + p
                row.append(p.astype(jnp.bfloat16))
            plan.append(jnp.concatenate(row, axis=1))
            m = m.T[:1, :]
            l = jnp.sum(l.T, axis=0, keepdims=True)
            copies(out_ref, k, m + jnp.log2(l))
            copies(out_ref, rows // LANE + k, m)
        plan = jnp.concatenate(plan, axis=0)
        total = jnp.dot(plan[:, :half], ya_ref[...], preferred_element_type=jnp.float32)
        total = total + jnp.dot(plan[:, half:], yb_ref[...], preferred_element_type=jnp.float32)
        here = pl.ds(b, BLK)
        held_ref[here, :] = total.astype(jnp.bfloat16)
        copy = pltpu.make_async_copy(held_ref.at[here], p_ref.at[here], sems.at[b // BLK])
        copy.start()
        leaving.append(copy)
    for copy in leaving:
        copy.wait()


def last_kernel(log2a, share, parts_ref, gain_ref, cand_ref, tgt_ref):
    top = share * lax.axis_size(CG) // LANE
    per = LANE // share
    per_xh = top // lax.axis_size("xh")
    mine = lax.axis_index(("xl", "y"))
    lane = lax.broadcasted_iota(jnp.int32, (1, LANE), 1) // share
    lse = merge(parts_ref[:, pl.ds(0, top), :])
    cand_ref[...] = jnp.zeros(cand_ref.shape, jnp.float32)
    row_of = lax.broadcasted_iota(jnp.int32, lse.shape, 0)

    def row(value, at):
        return jnp.sum(jnp.where(row_of == at, value, 0.0), axis=0, keepdims=True)

    def shifted(value, to, at):
        out = jnp.zeros_like(value)
        for off in range(per):
            moved = pltpu.roll(value, ((to - off) % per) * share, 1) if (to - off) % per else value
            out = jnp.where(at == off, moved, out)
        return out

    pieces = jnp.zeros((1, LANE), jnp.float32)
    for h in range(lax.axis_size("xh")):
        value = shifted(row(lse, h * per_xh + mine // per), h, lax.rem(mine, per))
        pieces = jnp.where(lane == h, value, pieces)
    cand_ref[pl.ds(lax.axis_index("z"), 1), :] = (log2a - pieces) / TO2

    me = lax.axis_index(CG)
    own = parts_ref[:, pl.ds(top + me // per, 1), :].reshape(parts_ref.shape[0], LANE)
    gain_ref[...] = shifted(jnp.exp2(own - row(lse, me // per)), 0, lax.rem(me, per))

    n = lax.axis_size(("xl", "y"))
    for k in range(n):
        pair = parts_ref[lax.axis_index("xh") * n + k, pl.ds(2 * top, 2), :]
        tgt_ref[pl.ds(2 * k, 2), :] = pair / TO2


VMEM = pl.BlockSpec(memory_space=pltpu.VMEM)
HBM = pl.BlockSpec(memory_space=pltpu.HBM)


def local(candidates, targets, target_domain, domain_counts):
    f32, bf16 = jnp.float32, jnp.bfloat16
    width = candidates.shape[1]
    plane = lax.axis_size(CG)
    pairs = lax.axis_size(TG)
    depth = lax.axis_size("z")
    share = candidates.shape[0]
    rows = share * plane
    half = targets.shape[0] * depth
    cols = 2 * half
    total_rows = rows * pairs
    total_cols = cols * plane

    def run(kernel, args, outs, scratch=(), special=(), cost=rows * cols):
        special = dict(special)
        return pl.pallas_call(
            kernel,
            in_specs=[special.get(i, VMEM) for i in range(len(args))],
            out_specs=[o[2] if len(o) > 2 else VMEM for o in outs],
            out_shape=[(pltpu.HBM if len(o) > 2 else jax.ShapeDtypeStruct)(o[0], o[1]) for o in outs],
            scratch_shapes=[pltpu.VMEM(*v) if isinstance(v, tuple) else v for v in scratch],
            compiler_params=pltpu.CompilerParams(vmem_limit_bytes=VMEM_LIMIT),
            cost_estimate=pl.CostEstimate(flops=cost * width, bytes_accessed=4 * cost, transcendentals=cost),
        )(*[pltpu.with_memory_space_constraint(a, pltpu.HBM) if special.get(i) is HBM else a for i, a in enumerate(args)])

    def shift(block, by):
        return lax.ppermute(block, "z", [(i, (i + by) % depth) for i in range(depth)])

    (x,) = run(
        spread_kernel,
        (candidates,),
        [((plane, share, width), bf16, HBM)],
        [pltpu.SemaphoreType.DMA((plane,))],
        cost=1,
    )
    x, targets = lax.optimization_barrier((x, targets))
    x = lax.all_to_all(x, CG, 0, 0, tiled=True).reshape(rows, width)
    counts = domain_counts.astype(f32)
    domains = jnp.arange(domain_counts.shape[0], dtype=jnp.int32)
    weight = jnp.sum(jnp.where(target_domain[:, None] == domains[None, :], counts[None, :], 0.0), axis=1)
    logb = jnp.log2(weight / jnp.sum(counts)) + (
        math.log2(domain_counts.shape[0]) - math.log2(total_cols)
    )
    mid = targets.shape[0] // 2
    two = [shift(targets, 2), shift(targets, -2)]
    far = [shift(two[0], 1), shift(two[1], -1)]
    late, *far = lax.optimization_barrier((targets, *far))
    near = [shift(late, 1), shift(late, -1)] + two
    ends = [shift(far[0][:mid], 1), shift(far[1][mid:], -1)]
    ya = jnp.concatenate([targets] + near + far + ends, axis=0)
    scale = TO2 / width
    ya, x, logb = lax.optimization_barrier((ya, x, logb[None, :]))
    yb = lax.ppermute(ya, "core", [(0, 1), (1, 0)])

    log2a = -math.log2(total_rows)
    row_shape = ((plane, rows // LANE, LANE), f32)
    col_shape = ((pairs, cols // LANE, LANE), f32)
    wide_shape = ((pairs, cols // LANE + 8, LANE), f32)
    last_shape = ((plane, 2 * rows // LANE + 8, LANE), f32)
    stat = ((rows, LANE), f32)
    vec = ((cols // LANE, LANE), f32)
    chalf = ((rows, half), f32)
    ca, m, l, sqx = run(functools.partial(first_cost, scale), (x, ya), [chalf, stat, stat, stat])
    cb, out = run(
        functools.partial(second_cost, scale), (x, sqx, yb, m, l), [chalf, row_shape], [stat, stat]
    )

    def columns(out, shape, *extra):
        parts = lax.all_to_all(out, CG, 0, 0, tiled=True)
        (out,) = run(functools.partial(col_kernel, log2a), (parts, ca, cb, *extra), [shape], [stat])
        return lax.all_to_all(out, TG, 0, 0, tiled=True)

    out, logb = run(
        row_kernel, (columns(out, wide_shape, logb), ca, cb), [row_shape, vec], [vec, vec, stat, stat]
    )
    out, partial = run(
        plan_kernel,
        (columns(out, col_shape), logb, ca, cb, ya, yb),
        [last_shape, ((rows, width), bf16, HBM)],
        [vec, vec, ((rows, width), bf16), pltpu.SemaphoreType.DMA((rows // BLK,))],
    )
    parts = lax.all_to_all(out, CG, 0, 0, tiled=True)
    moved = lax.all_to_all(partial.reshape(plane, share, width), CG, 0, 0, tiled=True)
    gain, cand, tgt = run(
        functools.partial(last_kernel, log2a, share),
        (parts,),
        [((plane, LANE), f32), ((depth, LANE), f32), vec],
    )
    projection = jnp.sum(moved.astype(f32) * gain[:, :share, None], axis=0).astype(bf16)
    for bit in (1, 2, 4):
        cand = cand + lax.ppermute(cand, "z", [(i, i ^ bit) for i in range(depth)])
    return projection, cand.reshape(-1), tgt.reshape(-1)


def solution(mesh):
    fine = Mesh(mesh.devices.reshape(2, -1, 2, mesh.shape["col"] // 2, 2), ROW + COL)
    tgt = P(COL + ROW)
    return jax.shard_map(
        local,
        mesh=fine,
        in_specs=(P(ROW + COL, None), P(COL + ROW, None), tgt, P()),
        out_specs=(P(ROW + COL, None), P(ROW), P(COL)),
        check_vma=False,
    )
```
